1024 devices in a mesh: ctx: 16 (over x, z_hi), exp: 64 (over y, z_lo, core).
Axes of the slice: x: 8, y: 8, z: 8 (z_hi: 2, z_lo: 4; z = z_hi * 4 + z_lo), core: 2. Of those that a mesh axis runs over, the one named last changes fastest.
Arguments:
- hidden_in: bfloat16 [1024, 4096], P('ctx'), may hold values from -0.59765625 to 0.59765625
- queries: bfloat16 [1024, 8192], P('ctx', 'exp'), may hold values from -120 to 120
- keys: bfloat16 [1024, 512], P('ctx'), may hold values from -6 to 6
- values: bfloat16 [1024, 512], P('ctx'), may hold values from -6 to 6
- out_proj: bfloat16 [8192, 4096], P('exp'), may hold values from -0.0625 to 0.0625
- norm_gain: float32 [4096], replicated, may hold values from 0.5 to 1.5
- routes: int32 [1024, 8], P('ctx'), may hold values from 0 to 63, all different within a row; in each aligned block of 64 rows (0 to 63, 64 to 127, ...) at most 16 rows name the same one
- gates: float32 [1024, 8], P('ctx'), may hold values from 0.05 to 0.3
- w_gate: bfloat16 [64, 4096, 1536], P('exp', None, 'ctx'), may hold values from -0.09375 to 0.09375
- w_up: bfloat16 [64, 4096, 1536], P('exp', None, 'ctx'), may hold values from -0.09375 to 0.09375
- w_down: bfloat16 [64, 1536, 4096], P('exp', 'ctx'), may hold values from -0.15625 to 0.15625
Outputs:
- layer_out: bfloat16 [1024, 4096], P(('ctx', 'exp'))
The draws below stay inside these ranges and needn't reach their ends.
Inputs may be any that keep to these rules, and one draw needn't show every extreme that they name: `routes`: each row names 8 distinct experts. Within each sequence shard's 64 rows no expert is named by more than 16 rows, a bound that some block reaches.
All inputs are finite; a program needn't handle non-finite values.
Results may differ from the reference program's by a relative error of at most 0.02.
Values may be sent and summed in bfloat16 or wider, within the bound.
A program may use at most 32 MiB of HBM per device.

```python
import math
import jax
import jax.numpy as jnp
import numpy as np
from jax import lax

D = 4096
HEADS = 64
KVH = 4
HD = 128
FF = 1536
TOP = 8
TOK_CTX = 64
TOKENS = 1024
EXPERTS = 64
CAPG = 16


def shared_keys(key):
    return jnp.clip(jax.random.normal(key, (TOKENS, KVH * HD), jnp.float32), -6.0, 6.0)


def draw_keys(key, part):
    key_base = shared_keys(key)
    return key_base.astype(jnp.bfloat16)


def draw_queries(key, part):
    key = jax.random.fold_in(key, 11)
    fresh_rows = jnp.clip(jax.random.normal(key, (TOKENS, HEADS * HD), jnp.float32), -6.0, 6.0)
    return fresh_rows.astype(jnp.bfloat16)


def steps_of(own_key, dims, split, smallest, largest):
    def one(dim, blocks):
        heights = jax.random.uniform(jax.random.fold_in(jax.random.fold_in(own_key, 6), dim), (blocks,), jnp.float32, smallest / len(split), largest / len(split))
        return jnp.repeat(jnp.exp(heights), dims[dim] // blocks).reshape((-1,) + (1,) * (len(dims) - dim - 1))

    level = one(*split[0])
    for cut in split[1:]:
        level = level * one(*cut)
    return level


def shared_out(rng, own, number, rows, number_of, top, bound, slope):
    ranking = jax.random.permutation(rng, number_of)
    crowded, ordinary = portions_of(number_of, rows * top, bound, slope, True), portions_of(number_of, rows * top, bound, slope, False)
    places = jnp.arange(number_of)

    def named(sizes, offset_by):
        used = int((sizes > 0).sum())
        fixed = max(1, used // 4)
        moved = fixed + (places - fixed + offset_by * (used - fixed)) % max(1, number_of - fixed)
        return jnp.zeros((number_of,), jnp.int32).at[ranking[jnp.where(places < fixed, places, moved)]].set(jnp.asarray(sizes, jnp.int32))

    sizes = jnp.where(number % 4 == 0, named(crowded, number // 4), named(ordinary, number - number // 4 - 1))
    mixed = jax.random.permutation(jax.random.fold_in(own, 3), number_of)
    source_of, sink = mixed[0:number_of // 2 * 2:2], mixed[1:number_of // 2 * 2:2]
    slack = jnp.minimum(sizes[source_of] - 1, bound - sizes[sink]) // 2
    slack = jnp.where((source_of == ranking[0]) | (sink == ranking[0]) | (sizes[sink] == 0), 0, jnp.maximum(slack, 0))
    moved = jax.random.randint(jax.random.fold_in(own, 4), (number_of // 2,), 0, 1 << 20) % (slack + 1)
    sizes = sizes.at[source_of].add(-moved).at[sink].add(moved)
    items = jnp.searchsorted(jnp.cumsum(sizes), jnp.arange(rows * top), side="right").astype(jnp.int32)
    listing = items.reshape(top, rows).T
    listing = listing[jax.random.permutation(jax.random.fold_in(own, 1), rows)]
    offset_by = jax.random.randint(jax.random.fold_in(own, 2), (rows, 1), 0, top)
    return jnp.take_along_axis(listing, (jnp.arange(top)[None, :] + offset_by) % top, axis=1)


def portions_of(count, total, limit, slope, full):
    weights = [(1 << 20) // math.isqrt(standing ** slope) + 1 for standing in range(1, count + 1)]
    largest = limit if full else min(limit, max(-(-total // count), total * weights[0] // sum(weights)))
    least = 1 if total - largest >= count - 1 else 0
    counts, surplus = [largest] + [least] * (count - 1), total - largest - least * (count - 1)
    while surplus > 0:
        candidates = [i for i in range(1, count) if counts[i] < largest] or [i for i in range(1, count) if counts[i] < limit]
        mass, left = sum([weights[i] for i in candidates]), surplus
        for i in candidates:
            extra = min(limit - counts[i], max(1, left * weights[i] // mass), surplus)
            counts[i] = counts[i] + extra
            surplus = surplus - extra
    return np.array(counts)


def centred(key, dims, spread, reach, shards=(), kind=jnp.bfloat16):
    level = steps_of(key, dims, shards, -0.22, 0.18) if shards else 1.0
    entries = jax.random.normal(key, dims, jnp.float32) * spread * level
    return jnp.minimum(jnp.maximum(entries, -reach), reach).astype(kind)


def setup_inputs(seed: int = 0) -> dict:
    key_list = jax.random.split(jax.random.key(seed), 12)
    hidden_in = centred(key_list[0], (TOKENS, D), 0.1, 0.59765625, ((0, 16),))
    queries = draw_queries(jax.random.fold_in(key_list[11], 71), 0)
    keys = draw_keys(jax.random.fold_in(key_list[11], 71), 0)
    values = centred(key_list[3], (TOKENS, KVH * HD), 1.0, 6.0, ((0, 16),))
    out_proj = centred(key_list[4], (HEADS * HD, D), (HEADS * HD) ** -0.5, 0.0625, ((0, 64),))
    norm_gain = jnp.clip(1.0 + 0.1 * jax.random.normal(key_list[5], (D,), jnp.float32), 0.5, 1.5)
    routes_keys = jax.random.split(jax.random.fold_in(key_list[6], 1), TOKENS // TOK_CTX)
    routes_turns = jax.random.permutation(jax.random.fold_in(key_list[6], 3), TOKENS // TOK_CTX)
    routes = jax.vmap(lambda own, number: shared_out(jax.random.fold_in(key_list[6], 2), own, number, TOK_CTX, EXPERTS, TOP, CAPG, 2))(routes_keys, routes_turns).reshape((TOKENS, TOP))
    gates = jnp.clip(jnp.exp(math.log(0.3) - 1.7917595 * jax.random.uniform(key_list[7], (TOKENS, TOP), jnp.float32) ** steps_of(key_list[7], (TOKENS, TOP), ((0, 16),), -0.2, 0.2)), 0.05, 0.3)
    w_gate = centred(key_list[8], (EXPERTS, D, FF), D ** -0.5, 0.09375, ((0, 64), (2, 16)))
    w_up = centred(key_list[9], (EXPERTS, D, FF), D ** -0.5, 0.09375, ((0, 64), (2, 16)))
    w_down = centred(key_list[10], (EXPERTS, FF, D), FF ** -0.5, 0.15625, ((0, 64), (1, 16)))
    return {"hidden_in": hidden_in, "queries": queries, "keys": keys, "values": values, "out_proj": out_proj, "norm_gain": norm_gain, "routes": routes, "gates": gates, "w_gate": w_gate, "w_up": w_up, "w_down": w_down}


highest = lax.Precision.HIGHEST

def reference(hidden_in, queries, keys, values, out_proj, norm_gain, routes, gates, w_gate, w_up, w_down):
    tokens = hidden_in.shape[0]
    group_size = HEADS // KVH
    position = jnp.arange(tokens, dtype=jnp.int32)
    causal = position[None, :] <= position[:, None]

    def one_head(head_index):
        kv_index = head_index // group_size
        query_h = lax.dynamic_slice_in_dim(queries, head_index * HD, HD, 1)
        key_h = lax.dynamic_slice_in_dim(keys, kv_index * HD, HD, 1)
        value_h = lax.dynamic_slice_in_dim(values, kv_index * HD, HD, 1)
        scores = lax.dot_general(query_h, key_h, (((1,), (1,)), ((), ())), preferred_element_type=jnp.float32) * HD ** (-0.5)
        masked = jnp.where(causal, scores, -jnp.inf)
        row_max = lax.optimization_barrier(jnp.max(masked, axis=1, keepdims=True))
        prob_raw = jnp.where(causal, jnp.exp(masked - row_max), 0.0)
        prob_sum = lax.optimization_barrier(jnp.sum(prob_raw, axis=1, keepdims=True))
        numerator = jnp.dot(prob_raw.astype(jnp.bfloat16), value_h, preferred_element_type=jnp.float32)
        return (numerator / prob_sum).astype(jnp.bfloat16)
    heads_out = lax.map(one_head, jnp.arange(HEADS, dtype=jnp.int32))
    attended = heads_out.transpose(1, 0, 2).reshape(tokens, HEADS * HD)
    mixed_all = hidden_in.astype(jnp.float32) + jnp.dot(attended, out_proj, preferred_element_type=jnp.float32)
    mean_square = lax.optimization_barrier(jnp.mean(mixed_all * mixed_all, axis=1, keepdims=True))
    normed = (mixed_all * lax.rsqrt(mean_square + 1e-06) * norm_gain).astype(jnp.bfloat16)
    groups = tokens // TOK_CTX
    unit_share = FF // groups
    slot_ids = jnp.arange(CAPG, dtype=jnp.int32)
    rows_grouped = normed.reshape(groups, TOK_CTX, D).astype(jnp.float32)

    def one_expert(expert_index, moe_sum):
        route_hit = routes == expert_index
        token_weight = lax.optimization_barrier(jnp.sum(jnp.where(route_hit, gates, 0.0), axis=1)).reshape(groups, TOK_CTX)
        member = jnp.any(route_hit, axis=1).reshape(groups, TOK_CTX)
        slot_index = jnp.cumsum(member.astype(jnp.int32), axis=1) - 1
        select = ((slot_index[:, None, :] == slot_ids[None, :, None]) & member[:, None, :]).astype(jnp.float32)
        picked = jnp.einsum('gct,gtd->gcd', select, rows_grouped, precision=highest).astype(jnp.bfloat16)
        picked = picked.reshape(groups * CAPG, D)
        gate_val = jnp.dot(picked, w_gate[expert_index], preferred_element_type=jnp.float32)
        up_val = jnp.dot(picked, w_up[expert_index], preferred_element_type=jnp.float32)
        act = (jax.nn.silu(gate_val) * up_val).astype(jnp.bfloat16)
        act_groups = act.reshape(groups * CAPG, groups, unit_share).astype(jnp.float32)
        down_groups = w_down[expert_index].reshape(groups, unit_share, D).astype(jnp.float32)
        parts = jnp.einsum('rsf,sfd->srd', act_groups, down_groups, precision=highest)
        rounded = lax.optimization_barrier(parts.astype(jnp.bfloat16)).astype(jnp.float32)
        expert_rows = lax.optimization_barrier(jnp.sum(rounded, axis=0)).reshape(groups, CAPG, D)
        slot_weight = jnp.einsum('gct,gt->gc', select, token_weight, precision=highest)
        back = jnp.einsum('gct,gcd->gtd', select, slot_weight[:, :, None] * expert_rows, precision=highest)
        return moe_sum + back.reshape(tokens, D)
    moe = lax.fori_loop(0, EXPERTS, one_expert, jnp.zeros((tokens, D), jnp.float32))
    return (mixed_all + moe).astype(jnp.bfloat16)
```

```python
import functools

import jax
import jax.numpy as jnp
from jax import lax
from jax.experimental import pallas as pl
from jax.experimental.pallas import tpu as pltpu
from jax.sharding import PartitionSpec as P

HEADS = 64
KVH = 4
SLOTS = 16
ZH, ZL, CO = 2, 4, 2
MESH = pl.DeviceIdType.MESH
F32, BF16 = jnp.float32, jnp.bfloat16
NT = (((1,), (1,)), ((), ()))
TN = (((0,), (0,)), ((), ()))


def kernel(
    nctx, nexp,
    hidden_in, queries, keys, values, out_proj, norm_gain, routes, gates, w_gate, w_up, w_down,
    out_ref,
    kv, qv, hid, wo, gain, rt, gt, wg, wu,
    pbuf, crecv, acc, rsy, acc2, rsz, ag,
    mt, wd, rows, act, act_t, oacc, expand, gated, r5c, acc5, r5y, acc6, r5z, snd, fin, own,
    lsem,
    s_kv, r_kv, s_kvc, r_kvc, s_sel, r_sel, s_wd, r_wd,
    s_c, r_c, s_y, r_y, s_z, r_z, s_gz, r_gz, s_gy, r_gy, s_gc, r_gc,
    s_zh, r_zh, s_ring, r_ring, s_azh, r_azh, s_aring, r_aring,
    s_5c, r_5c, s_5y, r_5y, s_5z, r_5z, s_f, r_f,
):
    nx, ny = nctx // ZH, nexp // (ZL * CO)
    tok, hd = qv.shape
    dim = hid.shape[1]
    ffs = w_down.shape[1]
    half = tok // 2
    dy, dz = dim // ny, dim // ny // ZL
    dc = dim // nctx
    c, e = lax.axis_index("ctx"), lax.axis_index("exp")
    x, zh = lax.div(c, ZH), lax.rem(c, ZH)
    y, zl, co = lax.div(e, ZL * CO), lax.rem(lax.div(e, CO), ZL), lax.rem(e, CO)
    core_e = e + 1 - 2 * co
    oco = 1 - co

    def ctx_at(xx, hh):
        return lax.rem(xx + nx, nx) * ZH + hh

    def exp_at(yy, zz, cc):
        return (yy * ZL + zz) * CO + cc

    sent = []

    def put(src, dst, ssem, rsem, cc, ee):
        copy = pltpu.make_async_remote_copy(
            src_ref=src, dst_ref=dst, send_sem=ssem, recv_sem=rsem,
            device_id=(cc, ee), device_id_type=MESH,
        )
        copy.start()
        sent.append(copy)
        return copy

    def landed(ref, rsem):
        pltpu.make_async_remote_copy(
            src_ref=ref, dst_ref=ref, send_sem=rsem, recv_sem=rsem,
            device_id=(c, core_e), device_id_type=MESH,
        ).wait_recv()

    def al(v, m):
        return pl.multiple_of(v, m)

    group = HEADS // KVH
    heads_here = max(1, HEADS // nexp)
    kv_col = al(lax.div(e * heads_here, group) * hd, hd)
    own_kv = kv.at[co, pl.ds(al(c * tok, tok), tok)]

    @pl.when(co == 0)
    def _():
        pltpu.make_async_copy(keys.at[:, pl.ds(kv_col, hd)], own_kv, lsem.at[0]).start()

    @pl.when(co == 1)
    def _():
        pltpu.make_async_copy(values.at[:, pl.ds(kv_col, hd)], own_kv, lsem.at[0]).start()

    own_wd = pltpu.make_async_copy(
        w_down.at[0, :, pl.ds(al(c * dc, dc), dc)], wd.at[pl.ds(al(c * ffs, ffs), ffs)], lsem.at[1]
    )
    loads = [
        pltpu.make_async_copy(src, dst, lsem.at[2 + i])
        for i, (src, dst) in enumerate([
            (routes, rt), (gates, gt), (queries, qv), (out_proj, wo), (hidden_in, hid),
            (norm_gain, gain), (w_gate.at[0], wg), (w_up.at[0], wu),
        ])
    ]
    for load in loads:
        load.start()
    own_wd.start()

    barrier = pltpu.get_barrier_semaphore()

    def greet(cc, ee):
        pl.semaphore_signal(barrier, inc=1, device_id=(cc, ee), device_id_type=MESH)

    for d in range(1, nctx):
        greet(lax.rem(c + d, nctx), e)
    for d in range(1, ny):
        greet(c, exp_at(lax.rem(y + d, ny), zl, co))
    for d in range(1, ZL):
        greet(c, exp_at(y, lax.rem(zl + d, ZL), co))
    greet(c, core_e)
    pl.semaphore_wait(barrier, (nctx - 1) + (ny - 1) + (ZL - 1) + 1)

    pltpu.make_async_copy(keys.at[:, pl.ds(kv_col, hd)], own_kv, lsem.at[0]).wait()
    for d in range(1, nctx):
        put(own_kv, own_kv, s_kv.at[d - 1], r_kv.at[d - 1], lax.rem(c + d, nctx), e)

    loads[0].wait()
    loads[1].wait()
    hit = rt[...] == e
    member = jnp.max(jnp.where(hit, 1.0, 0.0), axis=1, keepdims=True)
    weight = jnp.sum(jnp.where(hit, gt[...], 0.0), axis=1, keepdims=True)
    wide = mt.shape[1]
    t_row = lax.broadcasted_iota(jnp.int32, (tok, wide), 0)
    t_col = lax.broadcasted_iota(jnp.int32, (tok, wide), 1)
    same = jnp.where(t_row == t_col, 1.0, 0.0)
    upto = jnp.where(t_row <= t_col, 1.0, 0.0)
    member_r = jnp.sum(member * same, axis=0, keepdims=True)
    weight_r = jnp.sum(weight * same, axis=0, keepdims=True)
    count_r = jnp.sum(member * upto, axis=0, keepdims=True)
    slot_i = lax.broadcasted_iota(jnp.int32, (SLOTS, wide), 0).astype(F32)
    chosen = (count_r - 1.0 == slot_i) & (member_r > 0.0)
    own_mt = mt.at[pl.ds(al(c * SLOTS, SLOTS), SLOTS)]
    own_mt[...] = jnp.where(chosen, weight_r, 0.0)
    pick = jnp.where(chosen, 1.0, 0.0)
    mine = jnp.where(lax.broadcasted_iota(jnp.int32, (SLOTS, wide), 1) == e, 1.0, 0.0)
    pick2 = jnp.concatenate([pick, mine], axis=0)[:, :tok].astype(BF16)

    for d in range(1, nctx):
        src = lax.rem(c + nctx - d, nctx)
        landed(kv.at[co, pl.ds(al(src * tok, tok), tok)], r_kv.at[d - 1])
    put(kv.at[co], kv.at[co], s_kvc, r_kvc, c, core_e)
    for d in range(1, nctx):
        put(own_mt, own_mt, s_sel.at[d - 1], r_sel.at[d - 1], lax.rem(c + d, nctx), e)
    loads[2].wait()
    landed(kv.at[oco], r_kvc)

    scores = lax.dot_general(qv[...], kv[0], NT, preferred_element_type=F32) * hd ** (-0.5)
    n_keys = kv.shape[1]
    q_pos = c * tok + lax.broadcasted_iota(jnp.int32, (tok, n_keys), 0)
    visible = lax.broadcasted_iota(jnp.int32, (tok, n_keys), 1) <= q_pos
    masked = jnp.where(visible, scores, -1e30)
    prob = jnp.where(visible, jnp.exp(masked - jnp.max(masked, axis=1, keepdims=True)), 0.0)
    total = jnp.sum(prob, axis=1, keepdims=True)
    numer = jnp.dot(prob.astype(BF16), kv[1], preferred_element_type=F32)
    att = (numer / total).astype(BF16)
    loads[3].wait()
    for j in range(ny):
        cols = pl.ds(j * dy, dy)
        pbuf[:, cols] = jnp.dot(att, wo[:, cols], preferred_element_type=F32).astype(BF16)

    put(pbuf.at[pl.ds(al(oco * half, half), half)], crecv, s_c, r_c, c, core_e)
    for d in range(1, nctx):
        t = lax.rem(c + d, nctx)
        put(
            w_down.at[0, :, pl.ds(al(t * dc, dc), dc)], wd.at[pl.ds(al(c * ffs, ffs), ffs)],
            s_wd.at[d - 1], r_wd.at[d - 1], t, e,
        )
    landed(crecv, r_c)
    mine_rows = pl.ds(al(co * half, half), half)
    for j in range(ny):
        cols = pl.ds(j * dy, dy)
        acc[:, cols] = (pbuf[mine_rows, cols].astype(F32) + crecv[:, cols].astype(F32)).astype(BF16)
    for d in range(1, ny):
        t = lax.rem(y + d, ny)
        put(acc.at[:, pl.ds(al(t * dy, dy), dy)], rsy.at[d - 1], s_y.at[d - 1], r_y.at[d - 1], c, exp_at(t, zl, co))
    tot = acc[:, pl.ds(al(y * dy, dy), dy)].astype(F32)
    for d in range(1, ny):
        landed(rsy.at[d - 1], r_y.at[d - 1])
        tot = tot + rsy[d - 1].astype(F32)
    acc2[...] = tot.astype(BF16)
    for d in range(1, ZL):
        t = lax.rem(zl + d, ZL)
        put(acc2.at[:, pl.ds(al(t * dz, dz), dz)], rsz.at[d - 1], s_z.at[d - 1], r_z.at[d - 1], c, exp_at(y, t, co))
    tot = acc2[:, pl.ds(al(zl * dz, dz), dz)].astype(F32)
    for d in range(1, ZL):
        landed(rsz.at[d - 1], r_z.at[d - 1])
        tot = tot + rsz[d - 1].astype(F32)
    piece = pl.ds(al(y * dy + zl * dz, dz), dz)
    ag[mine_rows, piece] = tot.astype(BF16)
    for d in range(1, ZL):
        put(ag.at[mine_rows, piece], ag.at[mine_rows, piece], s_gz.at[d - 1], r_gz.at[d - 1], c, exp_at(y, lax.rem(zl + d, ZL), co))
    for d in range(1, ZL):
        src = lax.rem(zl + ZL - d, ZL)
        landed(ag.at[mine_rows, pl.ds(al(y * dy + src * dz, dz), dz)], r_gz.at[d - 1])
    piece = pl.ds(al(y * dy, dy), dy)
    for d in range(1, ny):
        put(ag.at[mine_rows, piece], ag.at[mine_rows, piece], s_gy.at[d - 1], r_gy.at[d - 1], c, exp_at(lax.rem(y + d, ny), zl, co))
    for d in range(1, ny):
        src = lax.rem(y + ny - d, ny)
        landed(ag.at[mine_rows, pl.ds(al(src * dy, dy), dy)], r_gy.at[d - 1])
    put(ag.at[mine_rows], ag.at[mine_rows], s_gc, r_gc, c, core_e)
    loads[4].wait()
    loads[5].wait()
    landed(ag.at[pl.ds(al(oco * half, half), half)], r_gc)

    square = jnp.zeros((SLOTS, 1), F32)
    mixes = []
    for j in range(ny):
        cols = pl.ds(j * dy, dy)
        mixed = jnp.dot(pick2, ag[:, cols], preferred_element_type=F32) + jnp.dot(
            pick2, hid[:, cols], preferred_element_type=F32
        )
        square = square + jnp.sum(mixed[:SLOTS] * mixed[:SLOTS], axis=1, keepdims=True)
        for k in range(dy // dc):
            own[j * (dy // dc) + k] = mixed[SLOTS : SLOTS + 1, k * dc : (k + 1) * dc]
        mixes.append(mixed[:SLOTS])
    scale = lax.rsqrt(square / dim + 1e-06)
    for j in range(ny):
        cols = pl.ds(j * dy, dy)
        rows[c, :, cols] = (mixes[j] * scale * gain[:, cols]).astype(BF16)

    hops = {(1, 0): nx // 2, (-1, 0): nx // 2 - 1, (1, 1): nx // 2 - 1, (-1, 1): nx // 2}
    first = {}
    n = 0
    for key in hops:
        first[key] = n
        n += hops[key]

    def ring(at, s_zh, r_zh, s_ring, r_ring, use):
        side = (zh, 1 - zh)

        def send(key, k):
            step, kind = key
            if k < hops[key]:
                ref = at(ctx_at(x - step * k, side[kind]))
                i = first[key] + k
                put(ref, ref, s_ring.at[i], r_ring.at[i], ctx_at(x + step, zh), e)

        def wait(key, k):
            step, kind = key
            block = ctx_at(x - step * k, side[kind])
            landed(at(block), r_ring.at[first[key] + k - 1])
            return block

        put(at(c), at(c), s_zh, r_zh, ctx_at(x, 1 - zh), e)
        send((1, 0), 0)
        send((-1, 0), 0)
        held = [c]
        for k in range(1, nx // 2 + 2):
            arrived = []
            for step in (1, -1):
                if k <= hops[(step, 0)]:
                    arrived.append(wait((step, 0), k))
                    send((step, 0), k)
            for step in (1, -1):
                if k == 1:
                    if step == 1:
                        partner = ctx_at(x, 1 - zh)
                        landed(at(partner), r_zh)
                        held.append(partner)
                    send((step, 1), 0)
                elif k - 1 <= hops[(step, 1)]:
                    held.append(wait((step, 1), k - 1))
                    send((step, 1), k - 1)
            use(held)
            held = arrived
        if held:
            use(held)

    for load in loads[6:]:
        load.wait()
    kc = dim // 4

    def expert(blocks):
        g = jnp.zeros((len(blocks) * SLOTS, ffs), F32)
        u = jnp.zeros((len(blocks) * SLOTS, ffs), F32)
        for k in range(4):
            part = pl.ds(k * kc, kc)
            rows_in = jnp.concatenate([rows[b, :, part] for b in blocks], axis=0)
            g = g + jnp.dot(rows_in, wg[part], preferred_element_type=F32)
            u = u + jnp.dot(rows_in, wu[part], preferred_element_type=F32)
        a = g / (1.0 + jnp.exp(-g)) * u
        for i, b in enumerate(blocks):
            act[pl.ds(al(b * SLOTS, SLOTS), SLOTS), :ffs] = a[i * SLOTS : (i + 1) * SLOTS]

    ring(lambda b: rows.at[b], s_zh, r_zh, s_ring, r_ring, expert)
    act_t[pl.ds(al(c * ffs, ffs), ffs), :] = act[...].T[:ffs].astype(BF16)

    for d in range(1, nctx):
        landed(mt.at[pl.ds(al(lax.rem(c + nctx - d, nctx) * SLOTS, SLOTS), SLOTS)], r_sel.at[d - 1])
    n_out = tok * nctx

    def place(i, _):
        blk = n_out // 8
        r = i * blk + lax.broadcasted_iota(jnp.int32, (blk, wide), 0)
        t = lax.broadcasted_iota(jnp.int32, (blk, wide), 1)
        p = lax.div(r, nctx)
        token = lax.rem(p, tok // CO) * CO + lax.div(p, tok // CO)
        pattern = jnp.where(t == token, 1.0, 0.0).astype(BF16)
        taken = jnp.where(mt[...] > 0.0, 1.0, 0.0).astype(BF16)
        hits = lax.dot_general(pattern, taken, NT, preferred_element_type=F32)
        r = i * blk + lax.broadcasted_iota(jnp.int32, hits.shape, 0)
        s = lax.broadcasted_iota(jnp.int32, hits.shape, 1)
        keep = lax.rem(r, nctx) == lax.div(s, SLOTS)
        expand[pl.ds(al(i * blk, blk), blk), :] = jnp.where(keep, hits, 0.0).astype(BF16)
        return 0

    lax.fori_loop(0, 8, place, 0)
    oacc[...] = jnp.zeros_like(oacc)
    own_wd.wait()
    for d in range(1, nctx):
        landed(wd.at[pl.ds(al(lax.rem(c + nctx - d, nctx) * ffs, ffs), ffs)], r_wd.at[d - 1])

    def down(blocks):
        tot = oacc[...]
        for b in blocks:
            part = pl.ds(al(b * ffs, ffs), ffs)
            tot = tot + lax.dot_general(act_t[part], wd[part], TN, preferred_element_type=F32)
        oacc[...] = tot

    ring(lambda b: act_t.at[pl.ds(al(b * ffs, ffs), ffs)], s_azh, r_azh, s_aring, r_aring, down)

    scaled = (oacc[...] * jnp.sum(mt[...], axis=1, keepdims=True)).astype(BF16)
    h5 = n_out // 2
    theirs = pl.ds(al(oco * h5, h5), h5)
    ours = pl.ds(al(co * h5, h5), h5)
    gated[theirs] = jnp.dot(expand[theirs], scaled, preferred_element_type=F32).astype(BF16)
    put(gated.at[theirs], r5c, s_5c, r_5c, c, core_e)
    gated[ours] = jnp.dot(expand[ours], scaled, preferred_element_type=F32).astype(BF16)
    landed(r5c, r_5c)
    acc5[...] = (gated[ours].astype(F32) + r5c[...].astype(F32)).astype(BF16)
    hy = h5 // ny
    for d in range(1, ny):
        t = lax.rem(y + d, ny)
        put(acc5.at[pl.ds(al(t * hy, hy), hy)], r5y.at[d - 1], s_5y.at[d - 1], r_5y.at[d - 1], c, exp_at(t, zl, co))
    tot = acc5[pl.ds(al(y * hy, hy), hy)].astype(F32)
    for d in range(1, ny):
        landed(r5y.at[d - 1], r_5y.at[d - 1])
        tot = tot + r5y[d - 1].astype(F32)
    acc6[...] = tot.astype(BF16)
    hz = hy // ZL
    for d in range(1, ZL):
        t = lax.rem(zl + d, ZL)
        put(acc6.at[pl.ds(al(t * hz, hz), hz)], r5z.at[d - 1], s_5z.at[d - 1], r_5z.at[d - 1], c, exp_at(y, t, co))
    tot = acc6[pl.ds(al(zl * hz, hz), hz)].astype(F32)
    for d in range(1, ZL):
        landed(r5z.at[d - 1], r_5z.at[d - 1])
        tot = tot + r5z[d - 1].astype(F32)

    for s in range(nctx):
        snd[s] = tot[s : s + 1]
    for d in range(1, nctx):
        t = lax.rem(c + d, nctx)
        put(snd.at[t], fin.at[c], s_f.at[d - 1], r_f.at[d - 1], t, e)
    fin[c] = snd[c]
    for d in range(1, nctx):
        landed(fin.at[lax.rem(c + nctx - d, nctx)], r_f.at[d - 1])
    out_ref[...] = own[...] + fin[...]
    for copy in sent:
        copy.wait_send()


def local(nctx, nexp, hidden_in, queries, keys, values, out_proj, norm_gain, routes, gates, w_gate, w_up, w_down):
    nx, ny = nctx // ZH, nexp // (ZL * CO)
    tok, hd = queries.shape
    dim = hidden_in.shape[1]
    ffs = w_down.shape[1]
    half = tok // 2
    dy, dz, dc = dim // ny, dim // ny // ZL, dim // nctx
    n_rows, n_out = nctx * SLOTS, nctx * tok
    wide = max(128, tok)
    ring = 4 * (nx // 2) - 2
    V, dma = pltpu.VMEM, pltpu.SemaphoreType.DMA
    pair = lambda n: [dma((n,)), dma((n,))] if n else [dma, dma]
    scratch = [
        V((2, nctx * tok, hd), BF16), V((tok, hd), BF16), V((tok, dim), BF16), V(out_proj.shape, BF16),
        V((1, dim), F32), V(routes.shape, jnp.int32), V(gates.shape, F32),
        V(w_gate.shape[1:], BF16), V(w_up.shape[1:], BF16),
        V((tok, dim), BF16), V((half, dim), BF16), V((half, dim), BF16), V((ny - 1, half, dy), BF16),
        V((half, dy), BF16), V((ZL - 1, half, dz), BF16), V((tok, dim), BF16),
        V((n_rows, wide), F32), V((nctx * ffs, dc), BF16), V((nctx, SLOTS, dim), BF16),
        V((n_rows, 128), F32), V((nctx * ffs, n_rows), BF16), V((n_rows, dc), F32),
        V((n_out, n_rows), BF16), V((n_out, dc), BF16), V((n_out // 2, dc), BF16), V((n_out // 2, dc), BF16),
        V((ny - 1, n_out // 2 // ny, dc), BF16), V((n_out // 2 // ny, dc), BF16), V((ZL - 1, nctx, dc), BF16),
        V((nctx, 1, dc), F32), V((nctx, 1, dc), F32), V((nctx, 1, dc), F32),
        dma((10,)),
        *pair(nctx - 1), *pair(0), *pair(nctx - 1), *pair(nctx - 1),
        *pair(0), *pair(ny - 1), *pair(ZL - 1), *pair(ZL - 1), *pair(ny - 1), *pair(0),
        *pair(0), *pair(ring), *pair(0), *pair(ring),
        *pair(0), *pair(ny - 1), *pair(ZL - 1), *pair(nctx - 1),
    ]
    out = pl.pallas_call(
        functools.partial(kernel, nctx, nexp),
        out_shape=jax.ShapeDtypeStruct((nctx, 1, dc), F32),
        in_specs=[pl.BlockSpec(memory_space=pl.ANY)] * 11,
        out_specs=pl.BlockSpec(memory_space=pltpu.VMEM),
        scratch_shapes=scratch,
        compiler_params=pltpu.CompilerParams(
            collective_id=0, has_side_effects=True, vmem_limit_bytes=40 * 1024 * 1024
        ),
        name="decoder_layer",
    )(hidden_in, queries, keys, values, out_proj, norm_gain.reshape(1, dim), routes, gates, w_gate, w_up, w_down)
    return out.reshape(1, dim).astype(BF16)


def solution(mesh):
    nctx, nexp = mesh.shape["ctx"], mesh.shape["exp"]
    return jax.shard_map(
        functools.partial(local, nctx, nexp),
        mesh=mesh,
        in_specs=(
            P("ctx", None),
            P("ctx", "exp"),
            P("ctx", None),
            P("ctx", None),
            P("exp", None),
            P(),
            P("ctx", None),
            P("ctx", None),
            P("exp", None, "ctx"),
            P("exp", None, "ctx"),
            P("exp", "ctx", None),
        ),
        out_specs=P(("ctx", "exp"), None),
        check_vma=False,
    )
```

```python
import functools

import jax
import jax.numpy as jnp
from jax import lax
from jax.experimental import pallas as pl
from jax.experimental.pallas import tpu as pltpu
from jax.sharding import PartitionSpec as P

HEADS = 64
KVH = 4
SLOTS = 16
ZH, ZL, CO = 2, 4, 2
PARTS = 4
MESH = pl.DeviceIdType.MESH
F32, BF16 = jnp.float32, jnp.bfloat16
NT = (((1,), (1,)), ((), ()))
TN = (((0,), (0,)), ((), ()))


def kernel(
    nctx, nexp,
    hidden_in, queries, keys, values, out_proj, norm_gain, routes, gates, w_gate, w_up, w_down,
    out_ref,
    kv, qv, hid, wo, gain, rt, gt, wgu,
    pbuf, crecv, acc, rsya, rsza, acca, rsyb, rszb, accb, ag,
    mt, wd, rows, act, oacc, expand, gated, r5c, acc5, r5ya, r5za, acc5a, r5yb, r5zb, acc5b, snd, fin, own,
    lsem,
    s_kv, r_kv, s_kvc, r_kvc, s_sel, r_sel, s_wd, r_wd,
    s_c, r_c, s_ya, r_ya, s_za, r_za, s_yb, r_yb, s_zb, r_zb,
    s_gya, r_gya, s_gza, r_gza, s_gyb, r_gyb, s_gzb, r_gzb, s_gc, r_gc,
    s_zh, r_zh, s_ring, r_ring, s_azh, r_azh, s_aring, r_aring,
    s_5c, r_5c, s_5ya, r_5ya, s_5za, r_5za, s_5yb, r_5yb, s_5zb, r_5zb, s_f, r_f,
):
    nx, ny = nctx // ZH, nexp // (ZL * CO)
    tok, hd = qv.shape
    dim = hid.shape[1]
    ffs = w_down.shape[1]
    half = tok // 2
    quarter = half // 2
    dp = dim // ny // ZL
    dc = dim // nctx
    lanes = act.shape[1] // nctx
    up_at = wgu.shape[0] // 2
    c, e = lax.axis_index("ctx"), lax.axis_index("exp")
    x, zh = lax.div(c, ZH), lax.rem(c, ZH)
    y, zl, co = lax.div(e, ZL * CO), lax.rem(lax.div(e, CO), ZL), lax.rem(e, CO)
    core_e = e + 1 - 2 * co
    oco = 1 - co

    def ctx_at(xx, hh):
        return lax.rem(xx + nx, nx) * ZH + hh

    def exp_at(yy, zz, cc):
        return (yy * ZL + zz) * CO + cc

    sent = []

    def put(src, dst, ssem, rsem, cc, ee):
        copy = pltpu.make_async_remote_copy(
            src_ref=src, dst_ref=dst, send_sem=ssem, recv_sem=rsem,
            device_id=(cc, ee), device_id_type=MESH,
        )
        copy.start()
        sent.append(copy)
        return copy

    def landed(ref, rsem):
        pltpu.make_async_remote_copy(
            src_ref=ref, dst_ref=ref, send_sem=rsem, recv_sem=rsem,
            device_id=(c, core_e), device_id_type=MESH,
        ).wait_recv()

    def al(v, m):
        return pl.multiple_of(v, m)

    def seg(i, n):
        return pl.ds(al(i * n, n), n)

    group = HEADS // KVH
    heads_here = max(1, HEADS // nexp)
    kv_col = al(lax.div(e * heads_here, group) * hd, hd)
    own_kv = kv.at[co, pl.ds(al(c * tok, tok), tok)]

    @pl.when(co == 0)
    def _():
        pltpu.make_async_copy(keys.at[:, pl.ds(kv_col, hd)], own_kv, lsem.at[0]).start()

    @pl.when(co == 1)
    def _():
        pltpu.make_async_copy(values.at[:, pl.ds(kv_col, hd)], own_kv, lsem.at[0]).start()

    own_wd = pltpu.make_async_copy(
        w_down.at[0, :, pl.ds(al(c * dc, dc), dc)], wd.at[c, :ffs], lsem.at[1]
    )
    loads = [
        pltpu.make_async_copy(src, dst, lsem.at[2 + i])
        for i, (src, dst) in enumerate([
            (routes, rt), (gates, gt), (queries, qv), (out_proj, wo), (hidden_in, hid),
            (norm_gain, gain), (w_gate.at[0], wgu.at[:ffs]), (w_up.at[0], wgu.at[pl.ds(up_at, ffs)]),
        ])
    ]
    for load in loads:
        load.start()
    own_wd.start()

    barrier = pltpu.get_barrier_semaphore()

    def greet(cc, ee):
        pl.semaphore_signal(barrier, inc=1, device_id=(cc, ee), device_id_type=MESH)

    for d in range(1, nctx):
        greet(lax.rem(c + d, nctx), e)
    for d in range(1, ny):
        greet(c, exp_at(lax.rem(y + d, ny), zl, co))
    for d in range(1, ZL):
        greet(c, exp_at(y, lax.rem(zl + d, ZL), co))
    greet(c, core_e)
    pl.semaphore_wait(barrier, (nctx - 1) + (ny - 1) + (ZL - 1) + 1)

    pltpu.make_async_copy(keys.at[:, pl.ds(kv_col, hd)], own_kv, lsem.at[0]).wait()
    def kv_at(block):
        return kv.at[co, pl.ds(al(block * tok, tok), tok)]

    partner = ctx_at(x, 1 - zh)
    for d in range(1, nctx):
        put(own_kv, own_kv, s_kv.at[d - 1], r_kv.at[d - 1], lax.rem(c + d, nctx), e)
    waiting = list(range(1, nctx))

    def some_down(count):
        for d in waiting[:count]:
            t = lax.rem(c + d, nctx)
            put(w_down.at[0, :, seg(t, dc)], wd.at[c, :ffs], s_wd.at[d - 1], r_wd.at[d - 1], t, e)
        del waiting[:count]

    some_down(15)

    if up_at > ffs:
        wgu[ffs:up_at] = jnp.zeros((up_at - ffs, dim), BF16)
        wgu[up_at + ffs :] = jnp.zeros((up_at - ffs, dim), BF16)
        wd[:, ffs:, :] = jnp.zeros((nctx, lanes - ffs, dc), BF16)

    loads[0].wait()
    loads[1].wait()
    hit = rt[...] == e
    member_r = jnp.max(jnp.where(hit, 1.0, 0.0), axis=0, keepdims=True)
    weight_r = jnp.sum(jnp.where(hit, gt[...], 0.0), axis=0, keepdims=True)
    wide = mt.shape[1]
    t_row = lax.broadcasted_iota(jnp.int32, (tok, tok), 0)
    t_col = lax.broadcasted_iota(jnp.int32, (tok, tok), 1)
    member = jnp.sum(jnp.where(t_row == t_col, member_r, 0.0), axis=1, keepdims=True)
    count_r = jnp.sum(jnp.where(t_row <= t_col, member, 0.0), axis=0, keepdims=True)
    if wide > tok:
        blank = jnp.zeros((1, wide - tok), F32)
        member_r = jnp.concatenate([member_r, blank], axis=1)
        weight_r = jnp.concatenate([weight_r, blank], axis=1)
        count_r = jnp.concatenate([count_r, blank], axis=1)
    slot_i = lax.broadcasted_iota(jnp.int32, (SLOTS, wide), 0).astype(F32)
    chosen = (count_r - 1.0 == slot_i) & (member_r > 0.0)
    own_mt = mt.at[pl.ds(al(c * SLOTS, SLOTS), SLOTS)]
    own_mt[...] = jnp.where(chosen, weight_r, 0.0).astype(BF16)
    pick = jnp.where(chosen, 1.0, 0.0)
    mine = jnp.where(lax.broadcasted_iota(jnp.int32, (SLOTS, wide), 1) == e, 1.0, 0.0)
    pick2 = jnp.concatenate([pick, mine], axis=0)[:, :tok].astype(BF16)

    for d in range(1, nctx):
        put(own_mt, own_mt, s_sel.at[d - 1], r_sel.at[d - 1], lax.rem(c + d, nctx), e)
    for d in range(1, nctx):
        landed(kv_at(lax.rem(c + nctx - d, nctx)), r_kv.at[d - 1])
    put(kv.at[co], kv.at[co], s_kvc, r_kvc, c, core_e)
    some_down(0)
    loads[2].wait()
    landed(kv.at[oco], r_kvc)

    scores = lax.dot_general(qv[...], kv[0], NT, preferred_element_type=F32) * hd ** (-0.5)
    n_keys = kv.shape[1]
    q_pos = c * tok + lax.broadcasted_iota(jnp.int32, (tok, n_keys), 0)
    visible = lax.broadcasted_iota(jnp.int32, (tok, n_keys), 1) <= q_pos
    masked = jnp.where(visible, scores, -1e30)
    prob = jnp.where(visible, jnp.exp(masked - jnp.max(masked, axis=1, keepdims=True)), 0.0)
    total = jnp.sum(prob, axis=1, keepdims=True)
    numer = jnp.dot(prob.astype(BF16), kv[1], preferred_element_type=F32)
    att = (numer / total).astype(BF16)
    loads[3].wait()
    n_col = 8
    dw = dim // n_col
    for j in range(n_col):
        cols = pl.ds(j * dw, dw)
        pbuf[:, cols] = jnp.dot(att, wo[:, cols], preferred_element_type=F32).astype(BF16)

    def across_y(d):
        return lax.rem(y + d, ny)

    def across_z(d):
        return lax.rem(zl + d, ZL)

    n_out = tok * nctx

    def place(i, _):
        blk = n_out // 8
        r = i * blk + lax.broadcasted_iota(jnp.int32, (blk, wide), 0)
        t = lax.broadcasted_iota(jnp.int32, (blk, wide), 1)
        p = lax.div(r, nctx)
        token = lax.rem(p, tok // CO) * CO + lax.div(p, tok // CO)
        pattern = jnp.where(t == token, 1.0, 0.0).astype(BF16)
        taken = jnp.where(mt[...].astype(F32) > 0.0, 1.0, 0.0).astype(BF16)
        hits = lax.dot_general(pattern, taken, NT, preferred_element_type=F32)
        r = i * blk + lax.broadcasted_iota(jnp.int32, hits.shape, 0)
        s = lax.broadcasted_iota(jnp.int32, hits.shape, 1)
        keep = lax.rem(r, nctx) == lax.div(s, SLOTS)
        expand[pl.ds(al(i * blk, blk), blk), :] = jnp.where(keep, hits, 0.0).astype(BF16)
        return 0

    def place_all():
        for d in range(1, nctx):
            landed(mt.at[seg(lax.rem(c + nctx - d, nctx), SLOTS)], r_sel.at[d - 1])
        lax.fori_loop(0, 8, place, 0)

    put(pbuf.at[pl.ds(al(oco * half, half), half)], crecv, s_c, r_c, c, core_e)
    some_down(0)
    landed(crecv, r_c)
    mine_rows = pl.ds(al(co * half, half), half)
    for j in range(n_col):
        cols = pl.ds(j * dw, dw)
        acc[:, cols] = (pbuf[mine_rows, cols].astype(F32) + crecv[:, cols].astype(F32)).astype(BF16)
    top, low = pl.ds(0, quarter), pl.ds(quarter, quarter)
    dya, dzb = dp * ZL, dp * ny

    for d in range(1, ny):
        t = across_y(d)
        put(acc.at[top, seg(t, dya)], rsya.at[d - 1], s_ya.at[d - 1], r_ya.at[d - 1], c, exp_at(t, zl, co))
    for d in range(1, ZL):
        t = across_z(d)
        put(acc.at[low, seg(t, dzb)], rszb.at[d - 1], s_zb.at[d - 1], r_zb.at[d - 1], c, exp_at(y, t, co))
    some_down(nctx)
    place_all()
    tot = acc[low, seg(zl, dzb)].astype(F32)
    for d in range(1, ZL):
        landed(rszb.at[d - 1], r_zb.at[d - 1])
        tot = tot + rszb[d - 1].astype(F32)
    accb[...] = tot.astype(BF16)
    for d in range(1, ny):
        t = across_y(d)
        put(accb.at[:, seg(t, dp)], rsyb.at[d - 1], s_yb.at[d - 1], r_yb.at[d - 1], c, exp_at(t, zl, co))
    tot = acc[top, seg(y, dya)].astype(F32)
    for d in range(1, ny):
        landed(rsya.at[d - 1], r_ya.at[d - 1])
        tot = tot + rsya[d - 1].astype(F32)
    acca[...] = tot.astype(BF16)
    for d in range(1, ZL):
        t = across_z(d)
        put(acca.at[:, seg(t, dp)], rsza.at[d - 1], s_za.at[d - 1], r_za.at[d - 1], c, exp_at(y, t, co))
    ag_top = pl.ds(al(co * half, quarter), quarter)
    ag_low = pl.ds(al(co * half + quarter, quarter), quarter)

    def cell(rows_at, at, n):
        return ag.at[rows_at, pl.ds(al(at, n), n)]

    tot = accb[:, seg(y, dp)].astype(F32)
    for d in range(1, ny):
        landed(rsyb.at[d - 1], r_yb.at[d - 1])
        tot = tot + rsyb[d - 1].astype(F32)
    own_b = cell(ag_low, zl * dzb + y * dp, dp)
    own_b[...] = tot.astype(BF16)
    for d in range(1, ny):
        put(own_b, own_b, s_gyb.at[d - 1], r_gyb.at[d - 1], c, exp_at(across_y(d), zl, co))
    tot = acca[:, seg(zl, dp)].astype(F32)
    for d in range(1, ZL):
        landed(rsza.at[d - 1], r_za.at[d - 1])
        tot = tot + rsza[d - 1].astype(F32)
    own_a = cell(ag_top, y * dya + zl * dp, dp)
    own_a[...] = tot.astype(BF16)
    for d in range(1, ZL):
        put(own_a, own_a, s_gza.at[d - 1], r_gza.at[d - 1], c, exp_at(y, across_z(d), co))
    for d in range(1, ZL):
        landed(cell(ag_top, y * dya + across_z(ZL - d) * dp, dp), r_gza.at[d - 1])
    line = cell(ag_top, y * dya, dya)
    for d in range(1, ny):
        put(line, line, s_gya.at[d - 1], r_gya.at[d - 1], c, exp_at(across_y(d), zl, co))
    for d in range(1, ny):
        landed(cell(ag_low, zl * dzb + across_y(ny - d) * dp, dp), r_gyb.at[d - 1])
    line = cell(ag_low, zl * dzb, dzb)
    for d in range(1, ZL):
        put(line, line, s_gzb.at[d - 1], r_gzb.at[d - 1], c, exp_at(y, across_z(d), co))
    for d in range(1, ZL):
        landed(cell(ag_low, across_z(ZL - d) * dzb, dzb), r_gzb.at[d - 1])
    for d in range(1, ny):
        landed(cell(ag_top, across_y(ny - d) * dya, dya), r_gya.at[d - 1])
    put(ag.at[mine_rows], ag.at[mine_rows], s_gc, r_gc, c, core_e)
    loads[4].wait()
    loads[5].wait()
    landed(ag.at[pl.ds(al(oco * half, half), half)], r_gc)

    square = jnp.zeros((SLOTS, 1), F32)
    mixes = []
    for j in range(n_col):
        cols = pl.ds(j * dw, dw)
        mixed = jnp.dot(pick2, ag[:, cols], preferred_element_type=F32) + jnp.dot(
            pick2, hid[:, cols], preferred_element_type=F32
        )
        square = square + jnp.sum(mixed[:SLOTS] * mixed[:SLOTS], axis=1, keepdims=True)
        own_part = mixed[SLOTS : SLOTS + 1]
        for k in range(max(1, dw // dc)):
            if dw >= dc:
                own[j * (dw // dc) + k] = own_part[:, k * dc : (k + 1) * dc]
            else:
                own[j * dw // dc, :, (j * dw) % dc : (j * dw) % dc + dw] = own_part
        mixes.append(mixed[:SLOTS])
    scale = lax.rsqrt(square / dim + 1e-06)
    for j in range(n_col):
        cols = pl.ds(j * dw, dw)
        rows[c, :, cols] = (mixes[j] * scale * gain[:, cols]).astype(BF16)

    far = nx // 2

    def route(parts, lag):
        hops, first, n = {}, {}, 0
        for kind in (0, 1):
            for h in range(parts):
                for step in (1, -1):
                    key = (step, kind, h)
                    most = far - 1 if lag and kind else far
                    hops[key] = far if (step == 1) == (h % 2 == 0) and most == far else far - 1
                    first[key] = n
                    n += hops[key]
        return hops, first

    side = (zh, 1 - zh)

    def ring_send(at, s_ring, r_ring, hops, first):
        def send(key, k):
            step, kind, h = key
            if k < hops[key]:
                ref = at(ctx_at(x - step * k, side[kind]), h)
                i = first[key] + k
                put(ref, ref, s_ring.at[i], r_ring.at[i], ctx_at(x + step, zh), e)

        return send

    def ring(at, parts, s_zh, r_zh, s_ring, r_ring, meanwhile, use, lag):
        hops, first = route(parts, lag)
        send = ring_send(at, s_ring, r_ring, hops, first)

        def wait(key, k):
            step, kind, h = key
            landed(at(ctx_at(x - step * k, side[kind]), h), r_ring.at[first[key] + k - 1])

        for h in range(parts):
            if lag:
                put(at(c, h), at(c, h), s_zh.at[h], r_zh.at[h], partner, e)
            for step in (1, -1):
                send((step, 0, h), 0)
        meanwhile()
        for k in range(1, far + 1 + lag):
            for h in range(parts):
                for step in (1, -1):
                    if k <= hops[(step, 0, h)]:
                        wait((step, 0, h), k)
                        send((step, 0, h), k)
                        if lag and k == far:
                            across = at(ctx_at(x - far, zh), h)
                            put(across, across, s_zh.at[parts + h], r_zh.at[parts + h], partner, e)
            m = k - lag
            for h in range(parts):
                if m == 0:
                    landed(at(partner, h), r_zh.at[h])
                if lag and m == far:
                    landed(at(ctx_at(x - far, 1 - zh), h), r_zh.at[parts + h])
                for step in (1, -1):
                    if 0 < m <= hops[(step, 1, h)]:
                        wait((step, 1, h), m)
                    if 0 <= m <= hops[(step, 1, h)]:
                        send((step, 1, h), m)
            use(k, m)

    def places(k):
        return [k] if k in (0, far) else [k, -k]

    def meanwhile():
        for load in loads[6:]:
            load.wait()

    kc = dim // 4

    def expert(k, m):
        spots = [lax.rem(x - i + nx, nx) for i in places(m)]
        blocks = [spot * ZH + h for spot in spots for h in range(ZH)]
        gu = jnp.zeros((len(blocks) * SLOTS, 2 * up_at), F32)
        for k in range(4):
            part = pl.ds(k * kc, kc)
            rows_in = jnp.concatenate([rows[b, :, part] for b in blocks], axis=0)
            gu = gu + lax.dot_general(rows_in, wgu[:, part], NT, preferred_element_type=F32)
        g, u = gu[:, :up_at], gu[:, up_at:]
        a = (g / (1.0 + jnp.exp(-g)) * u).astype(BF16)
        for i, b in enumerate(blocks):
            act[seg(b, SLOTS), seg(c, lanes)] = a[i * SLOTS : (i + 1) * SLOTS]
        for i, spot in zip(places(m), spots):
            piece = act.at[seg(spot, ZH * SLOTS), seg(c, lanes)]
            put(piece, piece, s_azh.at[i % nx], r_azh.at[i % nx], partner, e)

    dpart = dim // PARTS
    ring(
        lambda b, h: rows.at[b, :, pl.ds(h * dpart, dpart)],
        PARTS, s_zh, r_zh, s_ring, r_ring, meanwhile, expert, 1,
    )

    def add(blocks):
        tot = oacc[...]
        for b in blocks:
            tot = tot + jnp.dot(act[:, seg(b, lanes)], wd[b], preferred_element_type=F32)
        oacc[...] = tot

    n_half = nctx * SLOTS // 2

    earlier = list(sent)
    sent.clear()

    def from_partner():
        for i in range(nx):
            landed(act.at[seg(lax.rem(x + i, nx), ZH * SLOTS), seg(partner, lanes)], r_azh.at[(nx - i) % nx])
        for h in (0, 1):
            for step in (1, -1):
                relay((step, 1, h), 0)
        own_wd.wait()
        for d in range(1, nctx):
            landed(wd.at[lax.rem(c + nctx - d, nctx), :ffs], r_wd.at[d - 1])
        oacc[...] = jnp.zeros_like(oacc)
        add([c, partner])
        for copy in earlier:
            copy.wait_send()

    def down(k, m):
        add([ctx_at(x - i, h) for i in places(k) for h in range(ZH)])

    def act_at(b, h):
        return act.at[pl.ds(h * n_half, n_half), seg(b, lanes)]

    relay = ring_send(act_at, s_aring, r_aring, *route(2, 0))
    ring(act_at, 2, None, None, s_aring, r_aring, from_partner, down, 0)

    scaled = (oacc[...] * jnp.sum(mt[...].astype(F32), axis=1, keepdims=True)).astype(BF16)
    h5 = n_out // 2
    blocks5 = (ny, ZL, nctx, dc)

    def spread(side):
        return jnp.dot(expand[seg(side, h5)], scaled, preferred_element_type=F32).astype(BF16).reshape(blocks5)

    gated[oco] = spread(oco)
    put(gated.at[oco], r5c, s_5c, r_5c, c, core_e)
    gated[co] = spread(co)
    landed(r5c, r_5c)
    acc5[...] = (gated[co].astype(F32) + r5c[...].astype(F32)).astype(BF16)
    hc = dc // 2
    left, right = pl.ds(0, hc), pl.ds(hc, hc)
    for d in range(1, ny):
        t = across_y(d)
        put(acc5.at[t, :, :, left], r5ya.at[d - 1], s_5ya.at[d - 1], r_5ya.at[d - 1], c, exp_at(t, zl, co))
    for d in range(1, ZL):
        t = across_z(d)
        put(acc5.at[:, t, :, right], r5zb.at[d - 1], s_5zb.at[d - 1], r_5zb.at[d - 1], c, exp_at(y, t, co))
    tot = acc5[:, zl, :, right].astype(F32)
    for d in range(1, ZL):
        landed(r5zb.at[d - 1], r_5zb.at[d - 1])
        tot = tot + r5zb[d - 1].astype(F32)
    acc5b[...] = tot.astype(BF16)
    for d in range(1, ny):
        t = across_y(d)
        put(acc5b.at[t], r5yb.at[d - 1], s_5yb.at[d - 1], r_5yb.at[d - 1], c, exp_at(t, zl, co))
    tot = acc5[y, :, :, left].astype(F32)
    for d in range(1, ny):
        landed(r5ya.at[d - 1], r_5ya.at[d - 1])
        tot = tot + r5ya[d - 1].astype(F32)
    acc5a[...] = tot.astype(BF16)
    for d in range(1, ZL):
        t = across_z(d)
        put(acc5a.at[t], r5za.at[d - 1], s_5za.at[d - 1], r_5za.at[d - 1], c, exp_at(y, t, co))
    tot_b = acc5b[y].astype(F32)
    for d in range(1, ny):
        landed(r5yb.at[d - 1], r_5yb.at[d - 1])
        tot_b = tot_b + r5yb[d - 1].astype(F32)
    tot_a = acc5a[zl].astype(F32)
    for d in range(1, ZL):
        landed(r5za.at[d - 1], r_5za.at[d - 1])
        tot_a = tot_a + r5za[d - 1].astype(F32)
    tot = jnp.concatenate([tot_a, tot_b], axis=1)

    for s in range(nctx):
        snd[s] = tot[s : s + 1]
    for d in range(1, nctx):
        t = lax.rem(c + d, nctx)
        put(snd.at[t], fin.at[c], s_f.at[d - 1], r_f.at[d - 1], t, e)
    fin[c] = snd[c]
    for d in range(1, nctx):
        landed(fin.at[lax.rem(c + nctx - d, nctx)], r_f.at[d - 1])
    out_ref[...] = own[...] + fin[...]
    for copy in sent:
        copy.wait_send()


def local(nctx, nexp, hidden_in, queries, keys, values, out_proj, norm_gain, routes, gates, w_gate, w_up, w_down):
    nx, ny = nctx // ZH, nexp // (ZL * CO)
    tok, hd = queries.shape
    dim = hidden_in.shape[1]
    ffs = w_down.shape[1]
    half = tok // 2
    quarter = half // 2
    dp, dc = dim // ny // ZL, dim // nctx
    n_rows, n_out = nctx * SLOTS, nctx * tok
    wide = max(128, tok)
    lanes = -(-ffs // 128) * 128
    V, dma = pltpu.VMEM, pltpu.SemaphoreType.DMA
    pair = lambda n: [dma((n,)), dma((n,))] if n else [dma, dma]
    scratch = [
        V((2, nctx * tok, hd), BF16), V((tok, hd), BF16), V((tok, dim), BF16), V(out_proj.shape, BF16),
        V((1, dim), F32), V(routes.shape[::-1], jnp.int32), V(gates.shape[::-1], F32), V((2 * lanes, dim), BF16),
        V((tok, dim), BF16), V((half, dim), BF16), V((half, dim), BF16),
        V((ny - 1, quarter, dp * ZL), BF16), V((ZL - 1, quarter, dp), BF16), V((quarter, dp * ZL), BF16),
        V((ny - 1, quarter, dp), BF16), V((ZL - 1, quarter, dp * ny), BF16), V((quarter, dp * ny), BF16),
        V((tok, dim), BF16),
        V((n_rows, wide), BF16), V((nctx, lanes, dc), BF16), V((nctx, SLOTS, dim), BF16),
        V((n_rows, nctx * lanes), BF16), V((n_rows, dc), F32),
        V((n_out, n_rows), BF16), V((CO, ny, ZL, nctx, dc), BF16), V((ny, ZL, nctx, dc), BF16), V((ny, ZL, nctx, dc), BF16),
        V((ny - 1, ZL, nctx, dc // 2), BF16), V((ZL - 1, nctx, dc // 2), BF16), V((ZL, nctx, dc // 2), BF16),
        V((ny - 1, nctx, dc // 2), BF16), V((ZL - 1, ny, nctx, dc // 2), BF16), V((ny, nctx, dc // 2), BF16),
        V((nctx, 1, dc), F32), V((nctx, 1, dc), F32), V((nctx, 1, dc), F32),
        dma((10,)),
        *pair(nctx - 1), *pair(0), *pair(nctx - 1), *pair(nctx - 1),
        *pair(0), *pair(ny - 1), *pair(ZL - 1), *pair(ny - 1), *pair(ZL - 1),
        *pair(ny - 1), *pair(ZL - 1), *pair(ny - 1), *pair(ZL - 1), *pair(0),
        *pair(2 * PARTS), *pair(PARTS * (4 * (nx // 2) - 3)), *pair(nx), *pair(8 * (nx // 2) - 4),
        *pair(0), *pair(ny - 1), *pair(ZL - 1), *pair(ny - 1), *pair(ZL - 1), *pair(nctx - 1),
    ]
    out = pl.pallas_call(
        functools.partial(kernel, nctx, nexp),
        out_shape=jax.ShapeDtypeStruct((nctx, 1, dc), F32),
        in_specs=[pl.BlockSpec(memory_space=pl.ANY)] * 11,
        out_specs=pl.BlockSpec(memory_space=pltpu.VMEM),
        scratch_shapes=scratch,
        compiler_params=pltpu.CompilerParams(
            collective_id=0, has_side_effects=True, vmem_limit_bytes=60 * 1024 * 1024
        ),
        name="decoder_layer",
    )(
        hidden_in, queries, keys, values, out_proj, norm_gain.reshape(1, dim), routes.T, gates.T,
        jnp.swapaxes(w_gate, 1, 2), jnp.swapaxes(w_up, 1, 2), w_down,
    )
    return out.reshape(1, dim).astype(BF16)


def solution(mesh):
    nctx, nexp = mesh.shape["ctx"], mesh.shape["exp"]
    return jax.shard_map(
        functools.partial(local, nctx, nexp),
        mesh=mesh,
        in_specs=(
            P("ctx", None),
            P("ctx", "exp"),
            P("ctx", None),
            P("ctx", None),
            P("exp", None),
            P(),
            P("ctx", None),
            P("ctx", None),
            P("exp", None, "ctx"),
            P("exp", None, "ctx"),
            P("exp", "ctx", None),
        ),
        out_specs=P(("ctx", "exp"), None),
        check_vma=False,
    )
```

```python
import functools

import jax
import jax.numpy as jnp
from jax import lax
from jax.experimental import pallas as pl
from jax.experimental.pallas import tpu as pltpu
from jax.sharding import PartitionSpec as P

HEADS = 64
KVH = 4
SLOTS = 16
ZH, ZL, CO = 2, 4, 2
PARTS = 4
MESH = pl.DeviceIdType.MESH
F32, BF16 = jnp.float32, jnp.bfloat16
NT = (((1,), (1,)), ((), ()))
TN = (((0,), (0,)), ((), ()))


def kernel(
    nctx, nexp,
    hidden_in, queries, keys, values, out_proj, norm_gain, routes, gates, w_gate, w_up, w_down,
    out_ref,
    kv, qv, hid, wo, gain, rt, gt, wgu,
    pbuf, crecv, acc, rsya, rsza, acca, rsyb, rszb, accb, ag,
    mt, wd, rows, act, oacc, expand, gated, r5c, acc5, r5ya, r5za, acc5a, r5yb, r5zb, acc5b, snd, fin, own,
    lsem,
    s_kv, r_kv, s_kvc, r_kvc, s_sel, r_sel, s_wd, r_wd,
    s_c, r_c, s_ya, r_ya, s_za, r_za, s_yb, r_yb, s_zb, r_zb,
    s_gya, r_gya, s_gza, r_gza, s_gyb, r_gyb, s_gzb, r_gzb, s_gc, r_gc,
    s_zh, r_zh, s_ring, r_ring, s_azh, r_azh, s_aring, r_aring,
    s_5c, r_5c, s_5ya, r_5ya, s_5za, r_5za, s_5yb, r_5yb, s_5zb, r_5zb, s_f, r_f,
):
    nx, ny = nctx // ZH, nexp // (ZL * CO)
    tok, hd = qv.shape
    dim = hid.shape[1]
    ffs = w_down.shape[1]
    half = tok // 2
    quarter = half // 2
    dp = dim // ny // ZL
    dc = dim // nctx
    lanes = act.shape[1] // nctx
    up_at = wgu.shape[0] // 2
    c, e = lax.axis_index("ctx"), lax.axis_index("exp")
    x, zh = lax.div(c, ZH), lax.rem(c, ZH)
    y, zl, co = lax.div(e, ZL * CO), lax.rem(lax.div(e, CO), ZL), lax.rem(e, CO)
    core_e = e + 1 - 2 * co
    oco = 1 - co

    def ctx_at(xx, hh):
        return lax.rem(xx + nx, nx) * ZH + hh

    def exp_at(yy, zz, cc):
        return (yy * ZL + zz) * CO + cc

    sent = []

    def put(src, dst, ssem, rsem, cc, ee):
        copy = pltpu.make_async_remote_copy(
            src_ref=src, dst_ref=dst, send_sem=ssem, recv_sem=rsem,
            device_id=(cc, ee), device_id_type=MESH,
        )
        copy.start()
        sent.append(copy)
        return copy

    def landed(ref, rsem):
        pltpu.make_async_remote_copy(
            src_ref=ref, dst_ref=ref, send_sem=rsem, recv_sem=rsem,
            device_id=(c, core_e), device_id_type=MESH,
        ).wait_recv()

    def al(v, m):
        return pl.multiple_of(v, m)

    def seg(i, n):
        return pl.ds(al(i * n, n), n)

    group = HEADS // KVH
    heads_here = max(1, HEADS // nexp)
    kv_col = al(lax.div(e * heads_here, group) * hd, hd)
    own_kv = kv.at[co, pl.ds(al(c * tok, tok), tok)]

    @pl.when(co == 0)
    def _():
        pltpu.make_async_copy(keys.at[:, pl.ds(kv_col, hd)], own_kv, lsem.at[0]).start()

    @pl.when(co == 1)
    def _():
        pltpu.make_async_copy(values.at[:, pl.ds(kv_col, hd)], own_kv, lsem.at[0]).start()

    own_wd = pltpu.make_async_copy(
        w_down.at[0, :, pl.ds(al(c * dc, dc), dc)], wd.at[c, :ffs], lsem.at[1]
    )
    loads = [
        pltpu.make_async_copy(src, dst, lsem.at[2 + i])
        for i, (src, dst) in enumerate([
            (routes, rt), (gates, gt), (queries, qv), (out_proj, wo), (hidden_in, hid),
            (norm_gain, gain), (w_gate.at[0], wgu.at[:ffs]), (w_up.at[0], wgu.at[pl.ds(up_at, ffs)]),
        ])
    ]
    for load in loads:
        load.start()
    own_wd.start()

    barrier = pltpu.get_barrier_semaphore()

    def greet(cc, ee):
        pl.semaphore_signal(barrier, inc=1, device_id=(cc, ee), device_id_type=MESH)

    for d in range(1, nctx):
        greet(lax.rem(c + d, nctx), e)
    for d in range(1, ny):
        greet(c, exp_at(lax.rem(y + d, ny), zl, co))
    for d in range(1, ZL):
        greet(c, exp_at(y, lax.rem(zl + d, ZL), co))
    greet(c, core_e)
    pl.semaphore_wait(barrier, (nctx - 1) + (ny - 1) + (ZL - 1) + 1)

    pltpu.make_async_copy(keys.at[:, pl.ds(kv_col, hd)], own_kv, lsem.at[0]).wait()
    def kv_at(block):
        return kv.at[co, pl.ds(al(block * tok, tok), tok)]

    partner = ctx_at(x, 1 - zh)
    for d in range(1, nctx):
        put(own_kv, own_kv, s_kv.at[d - 1], r_kv.at[d - 1], lax.rem(c + d, nctx), e)
    waiting = list(range(1, nctx))

    def some_down(count):
        for d in waiting[:count]:
            t = lax.rem(c + d, nctx)
            put(w_down.at[0, :, seg(t, dc)], wd.at[c, :ffs], s_wd.at[d - 1], r_wd.at[d - 1], t, e)
        del waiting[:count]


    if up_at > ffs:
        wgu[ffs:up_at] = jnp.zeros((up_at - ffs, dim), BF16)
        wgu[up_at + ffs :] = jnp.zeros((up_at - ffs, dim), BF16)
        wd[:, ffs:, :] = jnp.zeros((nctx, lanes - ffs, dc), BF16)

    loads[0].wait()
    loads[1].wait()
    hit = rt[...] == e
    member_r = jnp.max(jnp.where(hit, 1.0, 0.0), axis=0, keepdims=True)
    weight_r = jnp.sum(jnp.where(hit, gt[...], 0.0), axis=0, keepdims=True)
    wide = mt.shape[1]
    t_row = lax.broadcasted_iota(jnp.int32, (tok, tok), 0)
    t_col = lax.broadcasted_iota(jnp.int32, (tok, tok), 1)
    member = jnp.sum(jnp.where(t_row == t_col, member_r, 0.0), axis=1, keepdims=True)
    count_r = jnp.sum(jnp.where(t_row <= t_col, member, 0.0), axis=0, keepdims=True)
    if wide > tok:
        blank = jnp.zeros((1, wide - tok), F32)
        member_r = jnp.concatenate([member_r, blank], axis=1)
        weight_r = jnp.concatenate([weight_r, blank], axis=1)
        count_r = jnp.concatenate([count_r, blank], axis=1)
    slot_i = lax.broadcasted_iota(jnp.int32, (SLOTS, wide), 0).astype(F32)
    chosen = (count_r - 1.0 == slot_i) & (member_r > 0.0)
    own_mt = mt.at[pl.ds(al(c * SLOTS, SLOTS), SLOTS)]
    own_mt[...] = jnp.where(chosen, weight_r, 0.0).astype(BF16)
    pick = jnp.where(chosen, 1.0, 0.0)
    mine = jnp.where(lax.broadcasted_iota(jnp.int32, (SLOTS, wide), 1) == e, 1.0, 0.0)
    pick2 = jnp.concatenate([pick, mine], axis=0)[:, :tok].astype(BF16)

    for d in range(1, nctx):
        put(own_mt, own_mt, s_sel.at[d - 1], r_sel.at[d - 1], lax.rem(c + d, nctx), e)
    some_down(8)
    for d in range(1, nctx):
        landed(kv_at(lax.rem(c + nctx - d, nctx)), r_kv.at[d - 1])
    put(kv.at[co], kv.at[co], s_kvc, r_kvc, c, core_e)
    some_down(4)
    loads[2].wait()
    landed(kv.at[oco], r_kvc)

    scores = lax.dot_general(qv[...], kv[0], NT, preferred_element_type=F32) * hd ** (-0.5)
    n_keys = kv.shape[1]
    q_pos = c * tok + lax.broadcasted_iota(jnp.int32, (tok, n_keys), 0)
    visible = lax.broadcasted_iota(jnp.int32, (tok, n_keys), 1) <= q_pos
    masked = jnp.where(visible, scores, -1e30)
    prob = jnp.where(visible, jnp.exp(masked - jnp.max(masked, axis=1, keepdims=True)), 0.0)
    total = jnp.sum(prob, axis=1, keepdims=True)
    numer = jnp.dot(prob.astype(BF16), kv[1], preferred_element_type=F32)
    att = (numer / total).astype(BF16)
    loads[3].wait()
    n_col = 8
    dw = dim // n_col
    for j in range(n_col):
        cols = pl.ds(j * dw, dw)
        pbuf[:, cols] = jnp.dot(att, wo[:, cols], preferred_element_type=F32).astype(BF16)

    def across_y(d):
        return lax.rem(y + d, ny)

    def across_z(d):
        return lax.rem(zl + d, ZL)

    n_out = tok * nctx

    def place(i, _):
        blk = n_out // 8
        r = i * blk + lax.broadcasted_iota(jnp.int32, (blk, wide), 0)
        t = lax.broadcasted_iota(jnp.int32, (blk, wide), 1)
        p = lax.div(r, nctx)
        token = lax.rem(p, tok // CO) * CO + lax.div(p, tok // CO)
        pattern = jnp.where(t == token, 1.0, 0.0).astype(BF16)
        taken = jnp.where(mt[...].astype(F32) > 0.0, 1.0, 0.0).astype(BF16)
        hits = lax.dot_general(pattern, taken, NT, preferred_element_type=F32)
        r = i * blk + lax.broadcasted_iota(jnp.int32, hits.shape, 0)
        s = lax.broadcasted_iota(jnp.int32, hits.shape, 1)
        keep = lax.rem(r, nctx) == lax.div(s, SLOTS)
        expand[pl.ds(al(i * blk, blk), blk), :] = jnp.where(keep, hits, 0.0).astype(BF16)
        return 0

    def place_all():
        for d in range(1, nctx):
            landed(mt.at[seg(lax.rem(c + nctx - d, nctx), SLOTS)], r_sel.at[d - 1])
        lax.fori_loop(0, 8, place, 0)

    put(pbuf.at[pl.ds(al(oco * half, half), half)], crecv, s_c, r_c, c, core_e)
    some_down(3)
    landed(crecv, r_c)
    mine_rows = pl.ds(al(co * half, half), half)
    for j in range(n_col):
        cols = pl.ds(j * dw, dw)
        acc[:, cols] = (pbuf[mine_rows, cols].astype(F32) + crecv[:, cols].astype(F32)).astype(BF16)
    top, low = pl.ds(0, quarter), pl.ds(quarter, quarter)
    dya, dzb = dp * ZL, dp * ny

    for d in range(1, ny):
        t = across_y(d)
        put(acc.at[top, seg(t, dya)], rsya.at[d - 1], s_ya.at[d - 1], r_ya.at[d - 1], c, exp_at(t, zl, co))
    for d in range(1, ZL):
        t = across_z(d)
        put(acc.at[low, seg(t, dzb)], rszb.at[d - 1], s_zb.at[d - 1], r_zb.at[d - 1], c, exp_at(y, t, co))
    some_down(nctx)
    place_all()
    tot = acc[low, seg(zl, dzb)].astype(F32)
    for d in range(1, ZL):
        landed(rszb.at[d - 1], r_zb.at[d - 1])
        tot = tot + rszb[d - 1].astype(F32)
    accb[...] = tot.astype(BF16)
    for d in range(1, ny):
        t = across_y(d)
        put(accb.at[:, seg(t, dp)], rsyb.at[d - 1], s_yb.at[d - 1], r_yb.at[d - 1], c, exp_at(t, zl, co))
    tot = acc[top, seg(y, dya)].astype(F32)
    for d in range(1, ny):
        landed(rsya.at[d - 1], r_ya.at[d - 1])
        tot = tot + rsya[d - 1].astype(F32)
    acca[...] = tot.astype(BF16)
    for d in range(1, ZL):
        t = across_z(d)
        put(acca.at[:, seg(t, dp)], rsza.at[d - 1], s_za.at[d - 1], r_za.at[d - 1], c, exp_at(y, t, co))
    ag_top = pl.ds(al(co * half, quarter), quarter)
    ag_low = pl.ds(al(co * half + quarter, quarter), quarter)

    def cell(rows_at, at, n):
        return ag.at[rows_at, pl.ds(al(at, n), n)]

    tot = accb[:, seg(y, dp)].astype(F32)
    for d in range(1, ny):
        landed(rsyb.at[d - 1], r_yb.at[d - 1])
        tot = tot + rsyb[d - 1].astype(F32)
    own_b = cell(ag_low, zl * dzb + y * dp, dp)
    own_b[...] = tot.astype(BF16)
    for d in range(1, ny):
        put(own_b, own_b, s_gyb.at[d - 1], r_gyb.at[d - 1], c, exp_at(across_y(d), zl, co))
    tot = acca[:, seg(zl, dp)].astype(F32)
    for d in range(1, ZL):
        landed(rsza.at[d - 1], r_za.at[d - 1])
        tot = tot + rsza[d - 1].astype(F32)
    own_a = cell(ag_top, y * dya + zl * dp, dp)
    own_a[...] = tot.astype(BF16)
    for d in range(1, ZL):
        put(own_a, own_a, s_gza.at[d - 1], r_gza.at[d - 1], c, exp_at(y, across_z(d), co))
    for d in range(1, ZL):
        landed(cell(ag_top, y * dya + across_z(ZL - d) * dp, dp), r_gza.at[d - 1])
    line = cell(ag_top, y * dya, dya)
    for d in range(1, ny):
        put(line, line, s_gya.at[d - 1], r_gya.at[d - 1], c, exp_at(across_y(d), zl, co))
    for d in range(1, ny):
        landed(cell(ag_low, zl * dzb + across_y(ny - d) * dp, dp), r_gyb.at[d - 1])
    line = cell(ag_low, zl * dzb, dzb)
    for d in range(1, ZL):
        put(line, line, s_gzb.at[d - 1], r_gzb.at[d - 1], c, exp_at(y, across_z(d), co))
    for d in range(1, ZL):
        landed(cell(ag_low, across_z(ZL - d) * dzb, dzb), r_gzb.at[d - 1])
    for d in range(1, ny):
        landed(cell(ag_top, across_y(ny - d) * dya, dya), r_gya.at[d - 1])
    put(ag.at[mine_rows], ag.at[mine_rows], s_gc, r_gc, c, core_e)
    loads[4].wait()
    loads[5].wait()
    landed(ag.at[pl.ds(al(oco * half, half), half)], r_gc)

    square = jnp.zeros((SLOTS, 1), F32)
    mixes = []
    for j in range(n_col):
        cols = pl.ds(j * dw, dw)
        mixed = jnp.dot(pick2, ag[:, cols], preferred_element_type=F32) + jnp.dot(
            pick2, hid[:, cols], preferred_element_type=F32
        )
        square = square + jnp.sum(mixed[:SLOTS] * mixed[:SLOTS], axis=1, keepdims=True)
        own_part = mixed[SLOTS : SLOTS + 1]
        for k in range(max(1, dw // dc)):
            if dw >= dc:
                own[j * (dw // dc) + k] = own_part[:, k * dc : (k + 1) * dc]
            else:
                own[j * dw // dc, :, (j * dw) % dc : (j * dw) % dc + dw] = own_part
        mixes.append(mixed[:SLOTS])
    scale = lax.rsqrt(square / dim + 1e-06)
    for j in range(n_col):
        cols = pl.ds(j * dw, dw)
        rows[c, :, cols] = (mixes[j] * scale * gain[:, cols]).astype(BF16)

    far = nx // 2

    def route(parts, lag):
        hops, first, n = {}, {}, 0
        for kind in (0, 1):
            for h in range(parts):
                for step in (1, -1):
                    key = (step, kind, h)
                    most = far - 1 if lag and kind else far
                    hops[key] = far if (step == 1) == (h % 2 == 0) and most == far else far - 1
                    first[key] = n
                    n += hops[key]
        return hops, first

    side = (zh, 1 - zh)

    def ring_send(at, s_ring, r_ring, hops, first):
        def send(key, k):
            step, kind, h = key
            if k < hops[key]:
                ref = at(ctx_at(x - step * k, side[kind]), h)
                i = first[key] + k
                put(ref, ref, s_ring.at[i], r_ring.at[i], ctx_at(x + step, zh), e)

        return send

    def ring(at, parts, s_zh, r_zh, s_ring, r_ring, meanwhile, use, lag):
        hops, first = route(parts, lag)
        send = ring_send(at, s_ring, r_ring, hops, first)

        def wait(key, k):
            step, kind, h = key
            landed(at(ctx_at(x - step * k, side[kind]), h), r_ring.at[first[key] + k - 1])

        for h in range(parts):
            if lag:
                put(at(c, h), at(c, h), s_zh.at[h], r_zh.at[h], partner, e)
            for step in (1, -1):
                send((step, 0, h), 0)
        meanwhile()
        for k in range(1, far + 1 + lag):
            for h in range(parts):
                for step in (1, -1):
                    if k <= hops[(step, 0, h)]:
                        wait((step, 0, h), k)
                        send((step, 0, h), k)
                        if lag and k == far:
                            across = at(ctx_at(x - far, zh), h)
                            put(across, across, s_zh.at[parts + h], r_zh.at[parts + h], partner, e)
            m = k - lag
            for h in range(parts):
                if m == 0:
                    landed(at(partner, h), r_zh.at[h])
                if lag and m == far:
                    landed(at(ctx_at(x - far, 1 - zh), h), r_zh.at[parts + h])
                for step in (1, -1):
                    if 0 < m <= hops[(step, 1, h)]:
                        wait((step, 1, h), m)
                    if 0 <= m <= hops[(step, 1, h)]:
                        send((step, 1, h), m)
            use(k, m)

    def places(k):
        return [k] if k in (0, far) else [k, -k]

    def meanwhile():
        for load in loads[6:]:
            load.wait()

    kc = dim // 4

    def expert(k, m):
        spots = [lax.rem(x - i + nx, nx) for i in places(m)]
        blocks = [spot * ZH + h for spot in spots for h in range(ZH)]
        gu = jnp.zeros((len(blocks) * SLOTS, 2 * up_at), F32)
        for k in range(4):
            part = pl.ds(k * kc, kc)
            rows_in = jnp.concatenate([rows[b, :, part] for b in blocks], axis=0)
            gu = gu + lax.dot_general(rows_in, wgu[:, part], NT, preferred_element_type=F32)
        g, u = gu[:, :up_at], gu[:, up_at:]
        a = (g / (1.0 + jnp.exp(-g)) * u).astype(BF16)
        for i, b in enumerate(blocks):
            act[seg(b, SLOTS), seg(c, lanes)] = a[i * SLOTS : (i + 1) * SLOTS]
        for i, spot in zip(places(m), spots):
            piece = act.at[seg(spot, ZH * SLOTS), seg(c, lanes)]
            put(piece, piece, s_azh.at[i % nx], r_azh.at[i % nx], partner, e)

    dpart = dim // PARTS
    ring(
        lambda b, h: rows.at[b, :, pl.ds(h * dpart, dpart)],
        PARTS, s_zh, r_zh, s_ring, r_ring, meanwhile, expert, 1,
    )

    def add(blocks):
        tot = oacc[...]
        for b in blocks:
            tot = tot + jnp.dot(act[:, seg(b, lanes)], wd[b], preferred_element_type=F32)
        oacc[...] = tot

    n_half = nctx * SLOTS // 2

    earlier = list(sent)
    sent.clear()

    def from_partner():
        for i in range(nx):
            landed(act.at[seg(lax.rem(x + i, nx), ZH * SLOTS), seg(partner, lanes)], r_azh.at[(nx - i) % nx])
        for h in (0, 1):
            for step in (1, -1):
                relay((step, 1, h), 0)
        own_wd.wait()
        for d in range(1, nctx):
            landed(wd.at[lax.rem(c + nctx - d, nctx), :ffs], r_wd.at[d - 1])
        oacc[...] = jnp.zeros_like(oacc)
        add([c, partner])
        for copy in earlier:
            copy.wait_send()

    def down(k, m):
        add([ctx_at(x - i, h) for i in places(k) for h in range(ZH)])

    def act_at(b, h):
        return act.at[pl.ds(h * n_half, n_half), seg(b, lanes)]

    relay = ring_send(act_at, s_aring, r_aring, *route(2, 0))
    ring(act_at, 2, None, None, s_aring, r_aring, from_partner, down, 0)

    scaled = (oacc[...] * jnp.sum(mt[...].astype(F32), axis=1, keepdims=True)).astype(BF16)
    h5 = n_out // 2
    blocks5 = (ny, ZL, nctx, dc)

    def spread(side):
        return jnp.dot(expand[seg(side, h5)], scaled, preferred_element_type=F32).astype(BF16).reshape(blocks5)

    gated[oco] = spread(oco)
    put(gated.at[oco], r5c, s_5c, r_5c, c, core_e)
    gated[co] = spread(co)
    landed(r5c, r_5c)
    acc5[...] = (gated[co].astype(F32) + r5c[...].astype(F32)).astype(BF16)
    hc = dc // 2
    left, right = pl.ds(0, hc), pl.ds(hc, hc)
    for d in range(1, ny):
        t = across_y(d)
        put(acc5.at[t, :, :, left], r5ya.at[d - 1], s_5ya.at[d - 1], r_5ya.at[d - 1], c, exp_at(t, zl, co))
    for d in range(1, ZL):
        t = across_z(d)
        put(acc5.at[:, t, :, right], r5zb.at[d - 1], s_5zb.at[d - 1], r_5zb.at[d - 1], c, exp_at(y, t, co))
    tot = acc5[:, zl, :, right].astype(F32)
    for d in range(1, ZL):
        landed(r5zb.at[d - 1], r_5zb.at[d - 1])
        tot = tot + r5zb[d - 1].astype(F32)
    acc5b[...] = tot.astype(BF16)
    for d in range(1, ny):
        t = across_y(d)
        put(acc5b.at[t], r5yb.at[d - 1], s_5yb.at[d - 1], r_5yb.at[d - 1], c, exp_at(t, zl, co))
    tot = acc5[y, :, :, left].astype(F32)
    for d in range(1, ny):
        landed(r5ya.at[d - 1], r_5ya.at[d - 1])
        tot = tot + r5ya[d - 1].astype(F32)
    acc5a[...] = tot.astype(BF16)
    for d in range(1, ZL):
        t = across_z(d)
        put(acc5a.at[t], r5za.at[d - 1], s_5za.at[d - 1], r_5za.at[d - 1], c, exp_at(y, t, co))
    tot_b = acc5b[y].astype(F32)
    for d in range(1, ny):
        landed(r5yb.at[d - 1], r_5yb.at[d - 1])
        tot_b = tot_b + r5yb[d - 1].astype(F32)
    tot_a = acc5a[zl].astype(F32)
    for d in range(1, ZL):
        landed(r5za.at[d - 1], r_5za.at[d - 1])
        tot_a = tot_a + r5za[d - 1].astype(F32)
    tot = jnp.concatenate([tot_a, tot_b], axis=1)

    for s in range(nctx):
        snd[s] = tot[s : s + 1]
    for d in range(1, nctx):
        t = lax.rem(c + d, nctx)
        put(snd.at[t], fin.at[c], s_f.at[d - 1], r_f.at[d - 1], t, e)
    fin[c] = snd[c]
    for d in range(1, nctx):
        landed(fin.at[lax.rem(c + nctx - d, nctx)], r_f.at[d - 1])
    out_ref[...] = own[...] + fin[...]
    for copy in sent:
        copy.wait_send()


def local(nctx, nexp, hidden_in, queries, keys, values, out_proj, norm_gain, routes, gates, w_gate, w_up, w_down):
    nx, ny = nctx // ZH, nexp // (ZL * CO)
    tok, hd = queries.shape
    dim = hidden_in.shape[1]
    ffs = w_down.shape[1]
    half = tok // 2
    quarter = half // 2
    dp, dc = dim // ny // ZL, dim // nctx
    n_rows, n_out = nctx * SLOTS, nctx * tok
    wide = max(128, tok)
    lanes = -(-ffs // 128) * 128
    V, dma = pltpu.VMEM, pltpu.SemaphoreType.DMA
    pair = lambda n: [dma((n,)), dma((n,))] if n else [dma, dma]
    scratch = [
        V((2, nctx * tok, hd), BF16), V((tok, hd), BF16), V((tok, dim), BF16), V(out_proj.shape, BF16),
        V((1, dim), F32), V(routes.shape[::-1], jnp.int32), V(gates.shape[::-1], F32), V((2 * lanes, dim), BF16),
        V((tok, dim), BF16), V((half, dim), BF16), V((half, dim), BF16),
        V((ny - 1, quarter, dp * ZL), BF16), V((ZL - 1, quarter, dp), BF16), V((quarter, dp * ZL), BF16),
        V((ny - 1, quarter, dp), BF16), V((ZL - 1, quarter, dp * ny), BF16), V((quarter, dp * ny), BF16),
        V((tok, dim), BF16),
        V((n_rows, wide), BF16), V((nctx, lanes, dc), BF16), V((nctx, SLOTS, dim), BF16),
        V((n_rows, nctx * lanes), BF16), V((n_rows, dc), F32),
        V((n_out, n_rows), BF16), V((CO, ny, ZL, nctx, dc), BF16), V((ny, ZL, nctx, dc), BF16), V((ny, ZL, nctx, dc), BF16),
        V((ny - 1, ZL, nctx, dc // 2), BF16), V((ZL - 1, nctx, dc // 2), BF16), V((ZL, nctx, dc // 2), BF16),
        V((ny - 1, nctx, dc // 2), BF16), V((ZL - 1, ny, nctx, dc // 2), BF16), V((ny, nctx, dc // 2), BF16),
        V((nctx, 1, dc), F32), V((nctx, 1, dc), F32), V((nctx, 1, dc), F32),
        dma((10,)),
        *pair(nctx - 1), *pair(0), *pair(nctx - 1), *pair(nctx - 1),
        *pair(0), *pair(ny - 1), *pair(ZL - 1), *pair(ny - 1), *pair(ZL - 1),
        *pair(ny - 1), *pair(ZL - 1), *pair(ny - 1), *pair(ZL - 1), *pair(0),
        *pair(2 * PARTS), *pair(PARTS * (4 * (nx // 2) - 3)), *pair(nx), *pair(8 * (nx // 2) - 4),
        *pair(0), *pair(ny - 1), *pair(ZL - 1), *pair(ny - 1), *pair(ZL - 1), *pair(nctx - 1),
    ]
    out = pl.pallas_call(
        functools.partial(kernel, nctx, nexp),
        out_shape=jax.ShapeDtypeStruct((nctx, 1, dc), F32),
        in_specs=[pl.BlockSpec(memory_space=pl.ANY)] * 11,
        out_specs=pl.BlockSpec(memory_space=pltpu.VMEM),
        scratch_shapes=scratch,
        compiler_params=pltpu.CompilerParams(
            collective_id=0, has_side_effects=True, vmem_limit_bytes=60 * 1024 * 1024
        ),
        name="decoder_layer",
    )(
        hidden_in, queries, keys, values, out_proj, norm_gain.reshape(1, dim), routes.T, gates.T,
        jnp.swapaxes(w_gate, 1, 2), jnp.swapaxes(w_up, 1, 2), w_down,
    )
    return out.reshape(1, dim).astype(BF16)


def solution(mesh):
    nctx, nexp = mesh.shape["ctx"], mesh.shape["exp"]
    return jax.shard_map(
        functools.partial(local, nctx, nexp),
        mesh=mesh,
        in_specs=(
            P("ctx", None),
            P("ctx", "exp"),
            P("ctx", None),
            P("ctx", None),
            P("exp", None),
            P(),
            P("ctx", None),
            P("ctx", None),
            P("exp", None, "ctx"),
            P("exp", None, "ctx"),
            P("exp", "ctx", None),
        ),
        out_specs=P(("ctx", "exp"), None),
        check_vma=False,
    )
```
